32 devices in a mesh: parts: 2 (over x), aux: 4 (over y, core), occ: 4 (over z).
Axes of the slice: x: 2, y: 2, z: 4, core: 2. Of those that a mesh axis runs over, the one named last changes fastest.
Arguments:
- three_center: bfloat16 [20480, 4, 2, 2048], P(('parts', 'aux'), 'occ'), parts along dimension 0, may hold values from -1.5 to 1.5
- tile_mask: int32 [8, 2, 32], P(('parts', 'occ')), parts along dimension 0, may hold values 0 or 1
- pair_orbitals: int32 [8, 2], P(('parts', 'occ')), parts along dimension 0, may hold values from 0 to 639
- occ_energy: float32 [1280], P('parts'), parts along dimension 0, may hold values from -1.2 to -0.3
- vir_energy: float32 [4096], P('parts'), parts along dimension 0, may hold values from 0.2 to 4
Outputs:
- gamma: bfloat16 [20480, 4, 2048], P(('parts', 'aux'), 'occ'), parts along dimension 0
- vir_density: float32 [4096, 2048], P(('parts', 'aux'), 'occ'), parts along dimension 0
The draws below stay inside these ranges and needn't reach their ends.
There are 2 independent parts, one for each index of `parts`. The reference program is written for one: setup_inputs(seed, part) draws one part's arguments, and reference() takes and returns one part's arrays. A program takes and returns all parts, laid end to end along the dimension named above; each array names one. Nothing has to cross between parts.
All inputs are finite; a program needn't handle non-finite values. No bound on the sum of `tile_mask` on one device may be relied on, other than what follows from the above.
Results may differ from the reference program's by a relative error of at most 0.014.
Values may be sent and summed in bfloat16 or wider, within the bound.
A program may use at most 192 MiB of HBM per device.

```python
import math
import jax
import jax.numpy as jnp
from jax import lax

NAUX = 10240
NVIR = 2048
NOCC = 640
TILE = 64
NPAIR = 4
NTILE = 32
N_AUX = 4


def with_ends(entries, rng, low, largest):
    extent = entries.shape
    index_at = [jax.random.randint(jax.random.fold_in(rng, axis), (), 0, extent[axis]) for axis in range(len(extent))]
    entries = entries.at[tuple(index_at)].set(low)
    longest = extent.index(max(extent))
    index_at[longest] = (index_at[longest] + 1) % extent[longest]
    return entries.at[tuple(index_at)].set(largest)


def levels(rng, shape, split, low, largest):
    level, own = 1.0, jax.random.fold_in(rng, 6)
    for position, blocks in split:
        steps = jnp.exp(jax.random.uniform(jax.random.fold_in(own, position), (blocks,), jnp.float32, low / len(split), largest / len(split)))
        level = level * jnp.repeat(steps, shape[position] // blocks).reshape([-1 if axis == position else 1 for axis in range(len(shape))])
    return level


def gaussian(rng, extent, spread, bound, shards=(), kind=jnp.bfloat16):
    result = spread * jax.random.normal(rng, extent, jnp.float32)
    if shards:
        result = result * levels(rng, extent, shards, -0.22, 0.18)
    return jnp.clip(result, -bound, bound).astype(kind)


def setup_inputs(seed: int = 0, part: int = 0) -> dict:
    key_of = jax.random.split(jax.random.key(seed), 6)
    part_splits = jax.random.split(jax.random.fold_in(key_of[5], part), 6)
    return {
        "three_center": gaussian(part_splits[0], (NAUX, NPAIR, 2, NVIR), (NAUX ** -0.25), 1.5, ((0, 4), (1, 4))),
        "tile_mask": with_ends((jax.random.randint(part_splits[1], (NPAIR, 2, NTILE), 0, 4) < 3).astype(jnp.int32), jax.random.fold_in(part_splits[1], 1), 0, 1),
        "pair_orbitals": with_ends(jax.random.randint(part_splits[2], (NPAIR, 2), 0, NOCC), jax.random.fold_in(part_splits[2], 1), 0, NOCC - 1).astype(jnp.int32),
        "occ_energy": jnp.clip(jax.random.uniform(part_splits[3], (NOCC,), jnp.float32, -1.2, -0.3), -1.2, -0.3),
        "vir_energy": jnp.clip(jnp.exp(jax.random.uniform(part_splits[4], (NVIR,), jnp.float32, math.log(0.2), math.log(4.0))), 0.2, 4.0),
    }


def reference(three_center, tile_mask, pair_orbitals, occ_energy, vir_energy):
    tile_keep = jnp.repeat(tile_mask, TILE, axis=2).astype(jnp.bfloat16)
    screened = three_center * tile_keep[None]
    q_block = NAUX // N_AUX

    def one_pair(index):
        first_orbital = screened[:, index, 0, :]
        second_orbital = screened[:, index, 1, :]
        first_blocks = first_orbital.reshape(N_AUX, q_block, NVIR)
        second_blocks = second_orbital.reshape(N_AUX, q_block, NVIR)

        def add_block(total, blocks):
            partial_sum = jnp.dot(blocks[0].T, blocks[1], preferred_element_type=jnp.float32)
            rounded = lax.optimization_barrier(partial_sum.astype(jnp.bfloat16))
            return total + rounded.astype(jnp.float32), None

        coulomb, _ = lax.scan(add_block, jnp.zeros((NVIR, NVIR), jnp.float32), (first_blocks, second_blocks))
        shift = occ_energy[pair_orbitals[index, 0]] + occ_energy[pair_orbitals[index, 1]]
        denominator = shift - vir_energy[:, None] - vir_energy[None, :]
        amplitude = (coulomb / denominator).astype(jnp.bfloat16)
        widened = amplitude.astype(jnp.float32)
        tilde = (2.0 * widened - widened.T).astype(jnp.bfloat16)
        gamma = jnp.dot(second_orbital, tilde.T, preferred_element_type=jnp.float32).astype(jnp.bfloat16)
        density = jnp.dot(amplitude, tilde.T, preferred_element_type=jnp.float32)
        return gamma, density

    gammas, densities = lax.map(one_pair, jnp.arange(NPAIR, dtype=jnp.int32))
    return jnp.transpose(gammas, (1, 0, 2)), jnp.sum(densities, axis=0)
```

```python
import jax
import jax.numpy as jnp
from jax import lax
from jax.sharding import PartitionSpec as P


def pick_shift(pair_orbitals, occ_energy):
    orbital_range = jnp.arange(occ_energy.shape[0], dtype=jnp.int32)
    matches = pair_orbitals[:, :, None] == orbital_range[None, None, :]
    picked = jnp.sum(jnp.where(matches, occ_energy[None, None, :], 0.0), axis=2)
    return picked[:, 0] + picked[:, 1]


def general_body(three_center, tile_mask, pair_orbitals, occ_energy, vir_energy):
    nvirt = three_center.shape[3]
    slab = nvirt // lax.axis_size("aux")
    width = nvirt // tile_mask.shape[2]
    tile_keep = jnp.repeat(tile_mask, width, axis=2).astype(jnp.bfloat16)
    screened = three_center * tile_keep[None]
    first_orbital = screened[:, :, 0, :]
    second_orbital = screened[:, :, 1, :]
    shift = pick_shift(pair_orbitals, occ_energy)
    offset = lax.axis_index("aux") * slab
    coulomb = lax.psum_scatter(
        jnp.einsum(
            "qpa,qpb->apb", first_orbital, second_orbital, preferred_element_type=jnp.float32
        ).astype(jnp.bfloat16),
        "aux",
        scatter_dimension=0,
        tiled=True,
    ).astype(jnp.float32)
    vir_rows = lax.dynamic_slice_in_dim(vir_energy, offset, slab, 0)
    denominator = shift[None, :, None] - vir_rows[:, None, None] - vir_energy[None, None, :]
    amplitude = (coulomb / denominator).astype(jnp.bfloat16)
    columns = lax.all_to_all(amplitude, "aux", split_axis=2, concat_axis=0, tiled=True)
    mirrored = jnp.transpose(columns, (2, 1, 0))
    tilde_part = (2.0 * amplitude.astype(jnp.float32) - mirrored.astype(jnp.float32)).astype(
        jnp.bfloat16
    )
    piece = lax.all_gather(tilde_part, "aux", axis=0, tiled=True)
    gamma_part = jnp.einsum(
        "qpb,apb->qpa", second_orbital, piece, preferred_element_type=jnp.float32
    )
    density_part = jnp.einsum("apc,bpc->ab", amplitude, piece, preferred_element_type=jnp.float32)
    vir_density = lax.psum_scatter(
        density_part.astype(jnp.bfloat16), "occ", scatter_dimension=1, tiled=True
    ).astype(jnp.float32)
    return (gamma_part.astype(jnp.bfloat16), vir_density)


SIBLING = [(0, 1), (1, 0), (2, 3), (3, 2)]
ACROSS = [(0, 2), (2, 0), (1, 3), (3, 1)]
CHUNKS = 4


def body(three_center, tile_mask, pair_orbitals, occ_energy, vir_energy):
    nvirt = three_center.shape[3]
    if lax.axis_size("aux") != 4 or three_center.shape[1] != 1 or nvirt % (CHUNKS * 512):
        return general_body(three_center, tile_mask, pair_orbitals, occ_energy, vir_energy)
    slab = nvirt // 4
    width = nvirt // tile_mask.shape[2]
    keep = jnp.repeat(tile_mask[0], width, axis=1).astype(jnp.float32)
    first = three_center[:, 0, 0, :]
    second = three_center[:, 0, 1, :]
    shift = pick_shift(pair_orbitals, occ_energy)[0]
    me = lax.axis_index("aux")
    core = lax.rem(me, 2)
    rows = nvirt // CHUNKS
    half = rows // 2
    amplitude = jnp.zeros((nvirt, nvirt), jnp.bfloat16)
    for k in range(CHUNKS):
        part = lax.dot_general(
            first[:, k * rows : (k + 1) * rows],
            second,
            (((0,), (0,)), ((), ())),
            preferred_element_type=jnp.float32,
        ).astype(jnp.bfloat16)
        mine = lax.dynamic_slice_in_dim(part, core * half, half, 0)
        other = lax.dynamic_slice_in_dim(part, (1 - core) * half, half, 0)
        got = lax.ppermute(other, "aux", SIBLING)
        chip = (mine.astype(jnp.float32) + got.astype(jnp.float32)).astype(jnp.bfloat16)
        far = lax.ppermute(chip, "aux", ACROSS)
        total = chip.astype(jnp.float32) + far.astype(jnp.float32)
        start = k * rows + core * half
        vir_rows = lax.dynamic_slice_in_dim(vir_energy, start, half, 0)
        keep_rows = lax.dynamic_slice_in_dim(keep[0], start, half, 0)
        denominator = shift - vir_rows[:, None] - vir_energy[None, :]
        amp = (total / denominator * keep_rows[:, None] * keep[1][None, :]).astype(jnp.bfloat16)
        amp_other = lax.ppermute(amp, "aux", SIBLING)
        amplitude = lax.dynamic_update_slice_in_dim(amplitude, amp, start, 0)
        amplitude = lax.dynamic_update_slice_in_dim(
            amplitude, amp_other, k * rows + (1 - core) * half, 0
        )
    wide = amplitude.astype(jnp.float32)
    tilde = ((2.0 * wide - wide.T) * keep[1][None, :]).astype(jnp.bfloat16)
    own = lax.dynamic_slice_in_dim(amplitude, me * slab, slab, 0)
    density_part = lax.dot_general(
        own, tilde, (((1,), (1,)), ((), ())), preferred_element_type=jnp.float32
    )
    vir_density = lax.psum_scatter(
        density_part.astype(jnp.bfloat16), "occ", scatter_dimension=1, tiled=True
    ).astype(jnp.float32)
    gamma = lax.dot_general(
        second, tilde, (((1,), (1,)), ((), ())), preferred_element_type=jnp.float32
    ).astype(jnp.bfloat16)
    return (gamma[:, None, :], vir_density)


def solution(mesh):
    in_specs = (
        P(("parts", "aux"), "occ", None, None),
        P(("parts", "occ"), None, None),
        P(("parts", "occ"), None),
        P("parts"),
        P("parts"),
    )
    out_specs = (P(("parts", "aux"), "occ", None), P(("parts", "aux"), "occ"))
    return jax.shard_map(body, mesh=mesh, in_specs=in_specs, out_specs=out_specs, check_vma=False)
```

```python
import jax
import jax.numpy as jnp
from jax import lax
from jax.experimental import pallas as pl
from jax.experimental.pallas import tpu as pltpu
from jax.sharding import PartitionSpec as P


def pick_shift(pair_orbitals, occ_energy):
    orbital_range = jnp.arange(occ_energy.shape[0], dtype=jnp.int32)
    matches = pair_orbitals[:, :, None] == orbital_range[None, None, :]
    picked = jnp.sum(jnp.where(matches, occ_energy[None, None, :], 0.0), axis=2)
    return picked[:, 0] + picked[:, 1]


def general_body(three_center, tile_mask, pair_orbitals, occ_energy, vir_energy):
    nvirt = three_center.shape[3]
    slab = nvirt // lax.axis_size("aux")
    width = nvirt // tile_mask.shape[2]
    tile_keep = jnp.repeat(tile_mask, width, axis=2).astype(jnp.bfloat16)
    screened = three_center * tile_keep[None]
    first_orbital = screened[:, :, 0, :]
    second_orbital = screened[:, :, 1, :]
    shift = pick_shift(pair_orbitals, occ_energy)
    offset = lax.axis_index("aux") * slab
    coulomb = lax.psum_scatter(
        jnp.einsum(
            "qpa,qpb->apb", first_orbital, second_orbital, preferred_element_type=jnp.float32
        ).astype(jnp.bfloat16),
        "aux",
        scatter_dimension=0,
        tiled=True,
    ).astype(jnp.float32)
    vir_rows = lax.dynamic_slice_in_dim(vir_energy, offset, slab, 0)
    denominator = shift[None, :, None] - vir_rows[:, None, None] - vir_energy[None, None, :]
    amplitude = (coulomb / denominator).astype(jnp.bfloat16)
    columns = lax.all_to_all(amplitude, "aux", split_axis=2, concat_axis=0, tiled=True)
    mirrored = jnp.transpose(columns, (2, 1, 0))
    tilde_part = (2.0 * amplitude.astype(jnp.float32) - mirrored.astype(jnp.float32)).astype(
        jnp.bfloat16
    )
    piece = lax.all_gather(tilde_part, "aux", axis=0, tiled=True)
    gamma_part = jnp.einsum(
        "qpb,apb->qpa", second_orbital, piece, preferred_element_type=jnp.float32
    )
    density_part = jnp.einsum("apc,bpc->ab", amplitude, piece, preferred_element_type=jnp.float32)
    vir_density = lax.psum_scatter(
        density_part.astype(jnp.bfloat16), "occ", scatter_dimension=1, tiled=True
    ).astype(jnp.float32)
    return (gamma_part.astype(jnp.bfloat16), vir_density)


SIBLING = [(0, 1), (1, 0), (2, 3), (3, 2)]
ACROSS = [(0, 2), (2, 0), (1, 3), (3, 1)]
CHUNKS = 8
VMEM = 56 * 1024 * 1024


def split_kernel(x_ref, first_ref, second_ref):
    block, width = first_ref.shape
    pairs = x_ref[...].reshape(2 * block, width)
    row = lax.broadcasted_iota(jnp.int32, (2 * block, 2 * block), 0)
    col = lax.broadcasted_iota(jnp.int32, (2 * block, 2 * block), 1)
    source = jnp.where(row < block, 2 * row, 2 * (row - block) + 1)
    order = (col == source).astype(jnp.bfloat16)
    both = jnp.dot(order, pairs, preferred_element_type=jnp.float32).astype(jnp.bfloat16)
    first_ref[...] = both[:block]
    second_ref[...] = both[block:]


def split_orbitals(three_center):
    naux, _, _, nvirt = three_center.shape
    block = 128
    return pl.pallas_call(
        split_kernel,
        grid=(naux // block,),
        in_specs=[pl.BlockSpec((block, 1, 2, nvirt), lambda i: (i, 0, 0, 0))],
        out_specs=[pl.BlockSpec((block, nvirt), lambda i: (i, 0))] * 2,
        out_shape=[jax.ShapeDtypeStruct((naux, nvirt), jnp.bfloat16)] * 2,
        compiler_params=pltpu.CompilerParams(vmem_limit_bytes=VMEM),
    )(three_center)


def tilde_kernel(me_ref, own_ref, rows_ref, cols_ref, keep_ref, tilde_ref, density_ref):
    slab, nvirt = rows_ref.shape
    for j in range(nvirt // slab):
        at = slice(j * slab, (j + 1) * slab)
        mirrored = cols_ref[at, :].T.astype(jnp.float32)
        value = 2.0 * rows_ref[:, at].astype(jnp.float32) - mirrored
        tilde_ref[:, at] = (value * keep_ref[:, at]).astype(jnp.bfloat16)
    density_ref[...] = lax.dot_general(
        own_ref[...],
        tilde_ref[...],
        (((1,), (1,)), ((), ())),
        preferred_element_type=jnp.float32,
    ).astype(jnp.bfloat16)


def tilde_density(me, amplitude, keep_row):
    nvirt = amplitude.shape[0]
    slab = nvirt // 4
    return pl.pallas_call(
        tilde_kernel,
        grid_spec=pltpu.PrefetchScalarGridSpec(
            num_scalar_prefetch=1,
            grid=(4,),
            in_specs=[
                pl.BlockSpec((slab, nvirt), lambda i, s: (s[0], 0)),
                pl.BlockSpec((slab, nvirt), lambda i, s: (i, 0)),
                pl.BlockSpec((nvirt, slab), lambda i, s: (0, i)),
                pl.BlockSpec((1, nvirt), lambda i, s: (0, 0)),
            ],
            out_specs=[
                pl.BlockSpec((slab, nvirt), lambda i, s: (i, 0)),
                pl.BlockSpec((slab, slab), lambda i, s: (0, i)),
            ],
        ),
        out_shape=[
            jax.ShapeDtypeStruct((nvirt, nvirt), jnp.bfloat16),
            jax.ShapeDtypeStruct((slab, nvirt), jnp.bfloat16),
        ],
        compiler_params=pltpu.CompilerParams(vmem_limit_bytes=VMEM),
    )(me.reshape(1), amplitude, amplitude, amplitude, keep_row)


def gamma_kernel(second_ref, tilde_ref, gamma_ref):
    gamma_ref[...] = lax.dot_general(
        second_ref[...],
        tilde_ref[...],
        (((1,), (1,)), ((), ())),
        preferred_element_type=jnp.float32,
    ).astype(jnp.bfloat16)


def gamma_of(second, tilde):
    naux, nvirt = second.shape
    block = 256
    return pl.pallas_call(
        gamma_kernel,
        grid=(naux // block,),
        in_specs=[
            pl.BlockSpec((block, nvirt), lambda i: (i, 0)),
            pl.BlockSpec((nvirt, nvirt), lambda i: (0, 0)),
        ],
        out_specs=pl.BlockSpec((block, nvirt), lambda i: (i, 0)),
        out_shape=jax.ShapeDtypeStruct((naux, nvirt), jnp.bfloat16),
        compiler_params=pltpu.CompilerParams(vmem_limit_bytes=VMEM),
        cost_estimate=pl.CostEstimate(
            flops=2 * naux * nvirt * nvirt,
            bytes_accessed=4 * naux * nvirt + 2 * nvirt * nvirt,
            transcendentals=0,
        ),
    )(second, tilde)


def body(three_center, tile_mask, pair_orbitals, occ_energy, vir_energy):
    naux, npair, _, nvirt = three_center.shape
    if lax.axis_size("aux") != 4 or npair != 1 or nvirt % (CHUNKS * 256) or naux % 256:
        return general_body(three_center, tile_mask, pair_orbitals, occ_energy, vir_energy)
    width = nvirt // tile_mask.shape[2]
    keep = jnp.repeat(tile_mask[0], width, axis=1).astype(jnp.float32)
    first, second = split_orbitals(three_center)
    shift = pick_shift(pair_orbitals, occ_energy)[0]
    me = lax.axis_index("aux")
    core = lax.rem(me, 2)
    rows = nvirt // CHUNKS
    half = rows // 2
    source = first
    chips = []
    fars = []
    for k in range(CHUNKS):
        if k >= 2:
            source, chips[k - 2] = lax.optimization_barrier((source, chips[k - 2]))
        part = lax.dot_general(
            source[:, k * rows : (k + 1) * rows],
            second,
            (((0,), (0,)), ((), ())),
            preferred_element_type=jnp.float32,
        ).astype(jnp.bfloat16)
        mine = lax.dynamic_slice_in_dim(part, core * half, half, 0)
        other = lax.dynamic_slice_in_dim(part, (1 - core) * half, half, 0)
        got = lax.ppermute(other, "aux", SIBLING)
        chips.append((mine.astype(jnp.float32) + got.astype(jnp.float32)).astype(jnp.bfloat16))
    amplitude = jnp.zeros((nvirt, nvirt), jnp.bfloat16)
    for k in range(CHUNKS):
        far = lax.ppermute(chips[k], "aux", ACROSS)
        total = chips[k].astype(jnp.float32) + far.astype(jnp.float32)
        start = k * rows + core * half
        vir_rows = lax.dynamic_slice_in_dim(vir_energy, start, half, 0)
        keep_rows = lax.dynamic_slice_in_dim(keep[0], start, half, 0)
        denominator = shift - vir_rows[:, None] - vir_energy[None, :]
        amp = (total / denominator * keep_rows[:, None] * keep[1][None, :]).astype(jnp.bfloat16)
        amp_other = lax.ppermute(amp, "aux", SIBLING)
        amplitude = lax.dynamic_update_slice_in_dim(amplitude, amp, start, 0)
        amplitude = lax.dynamic_update_slice_in_dim(
            amplitude, amp_other, k * rows + (1 - core) * half, 0
        )
    tilde, density_part = tilde_density(me, amplitude, keep[1:2])
    vir_density = lax.psum_scatter(
        density_part, "occ", scatter_dimension=1, tiled=True
    ).astype(jnp.float32)
    gamma = gamma_of(second, tilde)
    return (gamma[:, None, :], vir_density)


def solution(mesh):
    in_specs = (
        P(("parts", "aux"), "occ", None, None),
        P(("parts", "occ"), None, None),
        P(("parts", "occ"), None),
        P("parts"),
        P("parts"),
    )
    out_specs = (P(("parts", "aux"), "occ", None), P(("parts", "aux"), "occ"))
    return jax.shard_map(body, mesh=mesh, in_specs=in_specs, out_specs=out_specs, check_vma=False)
```

```python
import jax
import jax.numpy as jnp
from jax import lax
from jax.experimental import pallas as pl
from jax.experimental.pallas import tpu as pltpu
from jax.sharding import PartitionSpec as P


def pick_shift(pair_orbitals, occ_energy):
    orbital_range = jnp.arange(occ_energy.shape[0], dtype=jnp.int32)
    matches = pair_orbitals[:, :, None] == orbital_range[None, None, :]
    picked = jnp.sum(jnp.where(matches, occ_energy[None, None, :], 0.0), axis=2)
    return picked[:, 0] + picked[:, 1]


def general_body(three_center, tile_mask, pair_orbitals, occ_energy, vir_energy):
    nvirt = three_center.shape[3]
    slab = nvirt // lax.axis_size("aux")
    width = nvirt // tile_mask.shape[2]
    tile_keep = jnp.repeat(tile_mask, width, axis=2).astype(jnp.bfloat16)
    screened = three_center * tile_keep[None]
    first_orbital = screened[:, :, 0, :]
    second_orbital = screened[:, :, 1, :]
    shift = pick_shift(pair_orbitals, occ_energy)
    offset = lax.axis_index("aux") * slab
    coulomb = lax.psum_scatter(
        jnp.einsum(
            "qpa,qpb->apb", first_orbital, second_orbital, preferred_element_type=jnp.float32
        ).astype(jnp.bfloat16),
        "aux",
        scatter_dimension=0,
        tiled=True,
    ).astype(jnp.float32)
    vir_rows = lax.dynamic_slice_in_dim(vir_energy, offset, slab, 0)
    denominator = shift[None, :, None] - vir_rows[:, None, None] - vir_energy[None, None, :]
    amplitude = (coulomb / denominator).astype(jnp.bfloat16)
    columns = lax.all_to_all(amplitude, "aux", split_axis=2, concat_axis=0, tiled=True)
    mirrored = jnp.transpose(columns, (2, 1, 0))
    tilde_part = (2.0 * amplitude.astype(jnp.float32) - mirrored.astype(jnp.float32)).astype(
        jnp.bfloat16
    )
    piece = lax.all_gather(tilde_part, "aux", axis=0, tiled=True)
    gamma_part = jnp.einsum(
        "qpb,apb->qpa", second_orbital, piece, preferred_element_type=jnp.float32
    )
    density_part = jnp.einsum("apc,bpc->ab", amplitude, piece, preferred_element_type=jnp.float32)
    vir_density = lax.psum_scatter(
        density_part.astype(jnp.bfloat16), "occ", scatter_dimension=1, tiled=True
    ).astype(jnp.float32)
    return (gamma_part.astype(jnp.bfloat16), vir_density)


SIBLING = [(0, 1), (1, 0), (2, 3), (3, 2)]
ACROSS = [(0, 2), (2, 0), (1, 3), (3, 1)]
VMEM = 56 * 1024 * 1024


def split_kernel(x_ref, first_ref, second_ref):
    block, width = first_ref.shape
    pairs = x_ref[...].reshape(2 * block, width)
    row = lax.broadcasted_iota(jnp.int32, (2 * block, 2 * block), 0)
    col = lax.broadcasted_iota(jnp.int32, (2 * block, 2 * block), 1)
    source = jnp.where(row < block, 2 * row, 2 * (row - block) + 1)
    order = (col == source).astype(jnp.bfloat16)
    both = jnp.dot(order, pairs, preferred_element_type=jnp.float32).astype(jnp.bfloat16)
    first_ref[...] = both[:block]
    second_ref[...] = both[block:]


def split_orbitals(three_center):
    naux, _, _, nvirt = three_center.shape
    block = 128
    return pl.pallas_call(
        split_kernel,
        grid=(naux // block,),
        in_specs=[pl.BlockSpec((block, 1, 2, nvirt), lambda i: (i, 0, 0, 0))],
        out_specs=[pl.BlockSpec((block, nvirt), lambda i: (i, 0))] * 2,
        out_shape=[jax.ShapeDtypeStruct((naux, nvirt), jnp.bfloat16)] * 2,
        compiler_params=pltpu.CompilerParams(vmem_limit_bytes=VMEM),
    )(three_center)


def tilde_kernel(me_ref, own_ref, rows_ref, cols_ref, keep_ref, tilde_ref, density_ref):
    slab, nvirt = rows_ref.shape
    for j in range(nvirt // slab):
        at = slice(j * slab, (j + 1) * slab)
        mirrored = cols_ref[at, :].T.astype(jnp.float32)
        value = 2.0 * rows_ref[:, at].astype(jnp.float32) - mirrored
        tilde_ref[:, at] = (value * keep_ref[:, at]).astype(jnp.bfloat16)
    density_ref[...] = lax.dot_general(
        own_ref[...],
        tilde_ref[...],
        (((1,), (1,)), ((), ())),
        preferred_element_type=jnp.float32,
    ).astype(jnp.bfloat16)


def tilde_density(me, amplitude, keep_row):
    nvirt = amplitude.shape[0]
    slab = nvirt // 4
    return pl.pallas_call(
        tilde_kernel,
        grid_spec=pltpu.PrefetchScalarGridSpec(
            num_scalar_prefetch=1,
            grid=(4,),
            in_specs=[
                pl.BlockSpec((slab, nvirt), lambda i, s: (s[0], 0)),
                pl.BlockSpec((slab, nvirt), lambda i, s: (i, 0)),
                pl.BlockSpec((nvirt, slab), lambda i, s: (0, i)),
                pl.BlockSpec((1, nvirt), lambda i, s: (0, 0)),
            ],
            out_specs=[
                pl.BlockSpec((slab, nvirt), lambda i, s: (i, 0)),
                pl.BlockSpec((slab, slab), lambda i, s: (0, i)),
            ],
        ),
        out_shape=[
            jax.ShapeDtypeStruct((nvirt, nvirt), jnp.bfloat16),
            jax.ShapeDtypeStruct((slab, nvirt), jnp.bfloat16),
        ],
        compiler_params=pltpu.CompilerParams(vmem_limit_bytes=VMEM),
    )(me.reshape(1), amplitude, amplitude, amplitude, keep_row)


def gamma_kernel(second_ref, tilde_ref, gamma_ref):
    gamma_ref[...] = lax.dot_general(
        second_ref[...],
        tilde_ref[...],
        (((1,), (1,)), ((), ())),
        preferred_element_type=jnp.float32,
    ).astype(jnp.bfloat16)


def gamma_of(second, tilde):
    naux, nvirt = second.shape
    block = 256
    return pl.pallas_call(
        gamma_kernel,
        grid=(naux // block,),
        in_specs=[
            pl.BlockSpec((block, nvirt), lambda i: (i, 0)),
            pl.BlockSpec((nvirt, nvirt), lambda i: (0, 0)),
        ],
        out_specs=pl.BlockSpec((block, nvirt), lambda i: (i, 0)),
        out_shape=jax.ShapeDtypeStruct((naux, nvirt), jnp.bfloat16),
        compiler_params=pltpu.CompilerParams(vmem_limit_bytes=VMEM),
        cost_estimate=pl.CostEstimate(
            flops=2 * naux * nvirt * nvirt,
            bytes_accessed=4 * naux * nvirt + 2 * nvirt * nvirt,
            transcendentals=0,
        ),
    )(second, tilde)


def body(three_center, tile_mask, pair_orbitals, occ_energy, vir_energy):
    naux, npair, _, nvirt = three_center.shape
    if lax.axis_size("aux") != 4 or npair != 1 or nvirt % 2048 or naux % 256:
        return general_body(three_center, tile_mask, pair_orbitals, occ_energy, vir_energy)
    width = nvirt // tile_mask.shape[2]
    keep = jnp.repeat(tile_mask[0], width, axis=1).astype(jnp.float32)
    first, second = split_orbitals(three_center)
    shift = pick_shift(pair_orbitals, occ_energy)[0]
    me = lax.axis_index("aux")
    core = lax.rem(me, 2)
    unit = nvirt // 8
    spans = [(k * unit, (k + 1) * unit) for k in range(8)]
    source = first
    chips = []
    for k, (low, high) in enumerate(spans):
        half = (high - low) // 2
        if k >= 2:
            source, chips[k - 2] = lax.optimization_barrier((source, chips[k - 2]))
        part = lax.dot_general(
            source[:, low:high],
            second,
            (((0,), (0,)), ((), ())),
            preferred_element_type=jnp.float32,
        ).astype(jnp.bfloat16)
        mine = lax.dynamic_slice_in_dim(part, core * half, half, 0)
        other = lax.dynamic_slice_in_dim(part, (1 - core) * half, half, 0)
        got = lax.ppermute(other, "aux", SIBLING)
        chips.append((mine.astype(jnp.float32) + got.astype(jnp.float32)).astype(jnp.bfloat16))
    fars = [lax.ppermute(chip, "aux", ACROSS) for chip in chips]
    held = lax.optimization_barrier(tuple(fars[:6] + chips[6:]))
    fars[:6], chips[6:] = held[:6], held[6:]
    amplitude = jnp.zeros((nvirt, nvirt), jnp.bfloat16)
    for chip, far, (low, high) in zip(chips, fars, spans):
        half = (high - low) // 2
        start = low + core * half
        away = low + (1 - core) * half
        total = chip.astype(jnp.float32) + far.astype(jnp.float32)
        vir_rows = lax.dynamic_slice_in_dim(vir_energy, start, half, 0)
        keep_rows = lax.dynamic_slice_in_dim(keep[0], start, half, 0)
        denominator = shift - vir_rows[:, None] - vir_energy[None, :]
        amp = (total / denominator * keep_rows[:, None] * keep[1][None, :]).astype(jnp.bfloat16)
        amp_other = lax.ppermute(amp, "aux", SIBLING)
        amplitude = lax.dynamic_update_slice_in_dim(amplitude, amp, start, 0)
        amplitude = lax.dynamic_update_slice_in_dim(amplitude, amp_other, away, 0)
    tilde, density_part = tilde_density(me, amplitude, keep[1:2])
    vir_density = lax.psum_scatter(
        density_part, "occ", scatter_dimension=1, tiled=True
    ).astype(jnp.float32)
    gamma = gamma_of(second, tilde)
    return (gamma[:, None, :], vir_density)


def solution(mesh):
    in_specs = (
        P(("parts", "aux"), "occ", None, None),
        P(("parts", "occ"), None, None),
        P(("parts", "occ"), None),
        P("parts"),
        P("parts"),
    )
    out_specs = (P(("parts", "aux"), "occ", None), P(("parts", "aux"), "occ"))
    return jax.shard_map(body, mesh=mesh, in_specs=in_specs, out_specs=out_specs, check_vma=False)
```
